128 devices in a mesh: grp: 2 (over core), seq: 64 (over y, x, z).
Axes of the slice: x: 4, y: 4, z: 4, core: 2. Of those that a mesh axis runs over, the one named last changes fastest.
Arguments:
- queries: bfloat16 [131072, 2048], P(('grp', 'seq')), may hold values from -6 to 6
- keys: bfloat16 [131072, 2048], P(('grp', 'seq')), may hold values from -6 to 6
- values: bfloat16 [131072, 2048], P(('grp', 'seq')), may hold values from -6 to 6
- log_decay: float32 [16, 131072], P(None, ('grp', 'seq')), may hold values from -1 to 0
- out_gate: bfloat16 [131072, 2048], P(('grp', 'seq')), may hold values from -6 to 6
- norm_gain: float32 [2048], replicated, may hold values from 0.25 to 1.75
Outputs:
- attended: bfloat16 [131072, 2048], P(('grp', 'seq'))
The draws below stay inside these ranges and needn't reach their ends.
All inputs are finite; a program needn't handle non-finite values.
Results may differ from the reference program's by a relative error of at most 0.0052.
Values sent between devices are 32-bit elements; how exact they have to be, the bound alone decides.
No kernel may reach another device: no remote copies, remote signals or barrier semaphores. Data moves between devices by JAX's collectives and lax.ppermute only.
A program may use at most 320 MiB of HBM per device.

```python
import jax
import jax.numpy as jnp
from jax import lax

RESIDENT_HEADCNT = 16
HD = 128
TOK_DEV = 1024
SEQUENCE_SPAN = 131072


def draw_log_decay(key, part):
    key = jax.random.fold_in(key, 11)
    keys_list = jax.random.split(key, 7)
    slow_rate = jnp.exp(jax.random.uniform(keys_list[0], (RESIDENT_HEADCNT, 1), jnp.float32, jnp.log(0.1), jnp.log(0.5))) / SEQUENCE_SPAN
    fast_rate = jax.random.uniform(keys_list[1], (RESIDENT_HEADCNT, 1), jnp.float32, 1.0 / 50.0, 1.0 / 30.0)
    fast_share = 0.5
    fast = jax.random.uniform(keys_list[2], (RESIDENT_HEADCNT, 1), jnp.float32) < fast_share
    base = jnp.where(fast, fast_rate, slow_rate)
    blocks = SEQUENCE_SPAN // TOK_DEV
    factor = jnp.exp(jax.random.uniform(keys_list[3], (RESIDENT_HEADCNT, blocks), jnp.float32, jnp.log(0.5), jnp.log(2.0)))
    factor = jnp.repeat(factor, TOK_DEV, axis=1)
    jitter = jax.random.uniform(keys_list[4], (RESIDENT_HEADCNT, SEQUENCE_SPAN), jnp.float32, 0.5, 1.5)
    forgetting_speed = base * factor * jitter
    occurrence_indices = jax.random.randint(keys_list[5], (3, RESIDENT_HEADCNT), 0, SEQUENCE_SPAN)
    forgetting_penalty = jax.random.uniform(keys_list[6], (3, RESIDENT_HEADCNT), jnp.float32, 0.22, 0.4)
    occurrence_positions_list = jnp.arange(SEQUENCE_SPAN, dtype=jnp.int32)
    spike_occurrences = jnp.zeros((RESIDENT_HEADCNT, SEQUENCE_SPAN), jnp.float32)
    for chosen_attention_units in range(3):
        spike_occurrences = spike_occurrences + jnp.where(occurrence_positions_list[None, :] == occurrence_indices[chosen_attention_units][:, None], forgetting_penalty[chosen_attention_units][:, None], 0.0)
    return -(forgetting_speed + spike_occurrences)


def shard_levels(key, shape, cuts, least, high):
    def one(position, shards_of):
        draws = jax.random.uniform(jax.random.fold_in(jax.random.fold_in(key, 6), position), (shards_of,), jnp.float32, least / len(cuts), high / len(cuts))
        return jnp.repeat(jnp.exp(draws), shape[position] // shards_of).reshape((-1,) + (1,) * (len(shape) - position - 1))

    gain = one(*cuts[0])
    for cut in cuts[1:]:
        gain = gain * one(*cut)
    return gain


def centred(own_key, dims, scale, most, shards=(), kind=jnp.bfloat16):
    values = jax.random.normal(own_key, dims, jnp.float32) * scale
    if len(shards) > 0:
        values = shard_levels(own_key, dims, shards, -0.22, 0.18) * values
    return jnp.clip(values, min=-most, max=most).astype(kind)


def setup_inputs(seed: int = 0) -> dict:
    key_list = jax.random.split(jax.random.key(seed), 7)
    queries = centred(key_list[0], (SEQUENCE_SPAN, RESIDENT_HEADCNT * HD), 1.0, 6.0, ((0, 128),))
    keys = centred(key_list[1], (SEQUENCE_SPAN, RESIDENT_HEADCNT * HD), 1.0, 6.0, ((0, 128),))
    values = centred(key_list[2], (SEQUENCE_SPAN, RESIDENT_HEADCNT * HD), 1.0, 6.0, ((0, 128),))
    log_decay = draw_log_decay(jax.random.fold_in(key_list[6], 71), 0)
    out_gate = centred(key_list[4], (SEQUENCE_SPAN, RESIDENT_HEADCNT * HD), 1.0, 6.0, ((0, 128),))
    norm_gain = jnp.clip(1.0 + 0.15 * jax.random.normal(key_list[5], (RESIDENT_HEADCNT * HD,), jnp.float32), 0.25, 1.75)
    return dict(queries=queries, keys=keys, values=values, log_decay=log_decay, out_gate=out_gate, norm_gain=norm_gain)


def block_output(queries, keys, values, log_decay, out_gate, norm_gain, state):
    rows, feats = queries.shape
    heads = log_decay.shape[0]
    width = feats // heads
    q_three = queries.reshape(rows, heads, width).astype(jnp.float32)
    k_three = keys.reshape(rows, heads, width).astype(jnp.float32)
    v_three = values.reshape(rows, heads, width).astype(jnp.float32)
    cumul = jnp.cumsum(log_decay, axis=1)
    total = cumul[:, -1]
    scores = jnp.einsum('thd,shd->hts', q_three, k_three)
    gap = cumul[:, :, None] - cumul[:, None, :]
    occurrence_positions_list = jnp.arange(rows, dtype=jnp.int32)
    causal = occurrence_positions_list[:, None] >= occurrence_positions_list[None, :]
    weights = jnp.where(causal[None], jnp.exp(jnp.minimum(gap, 0.0)) * scores, 0.0).astype(jnp.bfloat16)
    weights = lax.optimization_barrier(weights)
    intra = jnp.einsum('hts,shd->thd', weights.astype(jnp.float32), v_three)
    rounded = lax.optimization_barrier(state.astype(jnp.bfloat16))
    inter = jnp.einsum('thd,hde->the', q_three, rounded.astype(jnp.float32))
    mixed = intra + jnp.exp(cumul).T[:, :, None] * inter
    power = lax.optimization_barrier(jnp.mean(mixed * mixed, axis=-1, keepdims=True))
    normed = mixed * lax.rsqrt(power + 1e-06) * norm_gain.reshape(heads, width)
    gate = out_gate.reshape(rows, heads, width).astype(jnp.float32)
    result = (normed * jax.nn.silu(gate)).astype(jnp.bfloat16).reshape(rows, feats)
    scaled_keys = (k_three * jnp.exp(total[None, :] - cumul.T)[:, :, None]).astype(jnp.bfloat16)
    scaled_keys = lax.optimization_barrier(scaled_keys)
    local_state = jnp.einsum('thd,the->hde', scaled_keys.astype(jnp.float32), v_three)
    return (result, total, local_state)

def reference(queries, keys, values, log_decay, out_gate, norm_gain):
    blocks = SEQUENCE_SPAN // TOK_DEV
    feats = queries.shape[1]
    q_blocks = queries.reshape(blocks, TOK_DEV, feats)
    k_blocks = keys.reshape(blocks, TOK_DEV, feats)
    v_blocks = values.reshape(blocks, TOK_DEV, feats)
    g_blocks = out_gate.reshape(blocks, TOK_DEV, feats)
    d_blocks = log_decay.reshape(RESIDENT_HEADCNT, blocks, TOK_DEV).transpose(1, 0, 2)

    def advance(state, inputs):
        q_part, k_part, v_part, d_part, g_part = inputs
        result, total, local_state = block_output(q_part, k_part, v_part, d_part, g_part, norm_gain, state)
        fresh = jnp.exp(total)[:, None, None] * state + local_state
        return (fresh, result)
    start = jnp.zeros((RESIDENT_HEADCNT, HD, HD), jnp.float32)
    _, results = lax.scan(advance, start, (q_blocks, k_blocks, v_blocks, d_blocks, g_blocks))
    return results.reshape(SEQUENCE_SPAN, feats)
```

```python
import functools

import jax
import jax.numpy as jnp
from jax import lax
from jax.experimental import pallas as pl
from jax.experimental.pallas import tpu as pltpu
from jax.sharding import PartitionSpec as P

AXES = ("grp", "seq")
MIB = 1 << 20
LOW = -1e30


def running_sum(decay):
    heads, rows = decay.shape
    a = lax.broadcasted_iota(jnp.int32, (128, 128), 0)
    b = lax.broadcasted_iota(jnp.int32, (128, 128), 1)
    upper = (a <= b).astype(jnp.float32)
    carry = jnp.zeros((heads, 1), jnp.float32)
    parts = []
    for c in range(rows // 128):
        part = jnp.dot(
            decay[:, c * 128 : (c + 1) * 128],
            upper,
            precision=lax.Precision.HIGHEST,
            preferred_element_type=jnp.float32,
        )
        part = part + carry
        carry = part[:, 127:128]
        parts.append(part)
    return jnp.concatenate(parts, axis=1)


def across(first, second):
    zero = jnp.zeros_like(first)
    return jnp.concatenate(
        [jnp.concatenate([first, zero], axis=1), jnp.concatenate([zero, second], axis=1)], axis=0
    )


def state_kernel(group, width, piece, tile, decay_ref, k_ref, v_ref, send_ref, near_ref, cumul_ref, sum_ref):
    step = pl.program_id(0)
    rows = k_ref.shape[0]

    @pl.when(step == 0)
    def _():
        cumul = running_sum(decay_ref[...])
        sum_ref[...] = cumul
        cumul_ref[...] = cumul

    per = width // piece
    parts = rows // tile
    for i in range(group):
        row = sum_ref[pl.ds(step * group + i, 1), :]
        cut = slice(i * width, (i + 1) * width)
        before = jnp.zeros((1, 1), jnp.float32)
        state = None
        for t in range(parts):
            mine = slice(t * tile, (t + 1) * tile)
            total = row[:, (t + 1) * tile - 1 : (t + 1) * tile]
            scale = jnp.exp(total - row[:, mine])
            keys = k_ref[mine, cut].T.astype(jnp.float32)
            scaled = (keys * scale).astype(jnp.bfloat16)
            fresh = jnp.dot(scaled, v_ref[mine, cut], preferred_element_type=jnp.float32)
            state = fresh if t == 0 else state * jnp.exp(total - before) + fresh
            before = total
            if t < parts - 1:
                at = (i * (parts - 1) + t) * width
                near_ref[at : at + width, :] = state.astype(jnp.bfloat16)
        factor = jnp.broadcast_to(jnp.exp(total), (8, width))
        for p in range(per):
            send_ref[i * per + p, 0:piece, :] = state[p * piece : (p + 1) * piece, :]
            send_ref[i * per + p, piece : piece + 8, :] = factor


def scan_kernel(piece, got_ref, out_ref):
    count = got_ref.shape[0]
    width = got_ref.shape[2]

    def lap(j, carry):
        out_ref[j, :, :] = carry
        factor = got_ref[j, piece : piece + 1, :]
        return carry * factor + got_ref[j, 0:piece, :]

    lax.fori_loop(0, count, lap, jnp.zeros((piece, width), jnp.float32), unroll=8)


def intra_kernel(group, width, tile, cumul_ref, near_ref, q_ref, k_ref, v_ref, out_ref):
    step = pl.program_id(0)
    rows = q_ref.shape[0]
    parts = rows // tile
    a = lax.broadcasted_iota(jnp.int32, (tile, tile), 0)
    b = lax.broadcasted_iota(jnp.int32, (tile, tile), 1)
    mask = jnp.where(a >= b, 0.0, LOW)
    for i in range(0, group, 2):
        row = [cumul_ref[pl.ds(step * group + i + n, 1), :] for n in range(2)]
        col = [jnp.broadcast_to(r, (8, rows)).T[:, 0:1] for r in row]
        both = slice(i * width, (i + 2) * width)
        for t in range(parts):
            start = t * tile
            mine = slice(start, start + tile)
            if t:
                at = [((i + n) * (parts - 1) + t - 1) * width for n in range(2)]
                far = jnp.dot(
                    q_ref[mine, both],
                    across(*(near_ref[x : x + width, :] for x in at)),
                    preferred_element_type=jnp.float32,
                )
            for n in range(2):
                cut = slice((i + n) * width, (i + n + 1) * width)
                scores = lax.dot_general(
                    q_ref[mine, cut],
                    k_ref[mine, cut],
                    (((1,), (1,)), ((), ())),
                    preferred_element_type=jnp.float32,
                )
                gap = col[n][mine] - row[n][:, mine] + mask
                weights = (jnp.exp(gap) * scores).astype(jnp.bfloat16)
                intra = jnp.dot(weights, v_ref[mine, cut], preferred_element_type=jnp.float32)
                if t:
                    edge = row[n][:, start - 1 : start]
                    intra = intra + jnp.exp(col[n][mine] - edge) * far[:, n * width : (n + 1) * width]
                out_ref[mine, cut] = intra.astype(out_ref.dtype)


def ready_kernel(group, width, cumul_ref, q_ref, gate_ref, gain_ref, scaled_ref, gated_ref):
    step = pl.program_id(0)
    rows = q_ref.shape[0]
    gate = gate_ref[...].astype(jnp.float32)
    gated = gain_ref[...] * (gate / (1.0 + jnp.exp(-gate)))
    gated_ref[...] = gated.astype(gated_ref.dtype)
    for i in range(group):
        cut = slice(i * width, (i + 1) * width)
        row = jnp.exp(cumul_ref[pl.ds(step * group + i, 1), :])
        col = jnp.broadcast_to(row, (8, rows)).T[:, 0:1]
        scaled_ref[:, cut] = (q_ref[:, cut].astype(jnp.float32) * col).astype(jnp.bfloat16)


def final_kernel(group, width, state_ref, q_ref, intra_ref, gated_ref, out_ref):
    share = jnp.full((width, width), 1.0 / width, jnp.bfloat16)
    share = across(share, share)
    for i in range(0, group, 2):
        both = slice(i * width, (i + 2) * width)
        state = state_ref[i * width : (i + 2) * width, :].astype(jnp.bfloat16)
        mixed = intra_ref[:, both].astype(jnp.float32) + jnp.dot(
            q_ref[:, both],
            across(state[0:width], state[width:]),
            preferred_element_type=jnp.float32,
        )
        power = jnp.dot(
            (mixed * mixed).astype(jnp.bfloat16), share, preferred_element_type=jnp.float32
        )
        out = mixed * lax.rsqrt(power + 1e-6) * gated_ref[:, both].astype(jnp.float32)
        out_ref[:, both] = out.astype(jnp.bfloat16)


def on_device(count, queries, keys, values, log_decay, out_gate, norm_gain):
    rows, feats = queries.shape
    heads = log_decay.shape[0]
    width = feats // heads
    piece = heads * width // count
    tile = 256
    parts = rows // tile
    f32, bf16 = jnp.float32, jnp.bfloat16

    def whole(*shape):
        return pl.BlockSpec(shape, lambda s: (0,) * len(shape))

    def cols(group):
        return pl.BlockSpec((rows, group * width), lambda s: (0, s))

    def lines(n):
        return pl.BlockSpec((n, width), lambda s: (s, 0))

    def gain(group):
        return pl.BlockSpec((1, group * width), lambda s: (0, s))

    def like(dtype):
        return jax.ShapeDtypeStruct((rows, feats), dtype)

    def call(name, body, group, ins, outs, shapes, flops, moved, exps, scratch=()):
        return pl.pallas_call(
            body,
            grid=(heads // group,),
            in_specs=ins,
            out_specs=outs,
            out_shape=shapes,
            scratch_shapes=list(scratch),
            compiler_params=pltpu.CompilerParams(vmem_limit_bytes=60 * MIB),
            cost_estimate=pl.CostEstimate(flops=flops, bytes_accessed=moved, transcendentals=exps),
            name=name,
        )

    group = 4
    send, near, cumul = call(
        "states",
        functools.partial(state_kernel, group, width, piece, tile),
        group,
        [whole(heads, rows), cols(group), cols(group)],
        [
            pl.BlockSpec((group * width // piece, piece + 8, width), lambda s: (s, 0, 0)),
            lines(group * (parts - 1) * width),
            whole(heads, rows),
        ],
        [
            jax.ShapeDtypeStruct((count, piece + 8, width), f32),
            jax.ShapeDtypeStruct((heads * (parts - 1) * width, width), bf16),
            jax.ShapeDtypeStruct((heads, rows), f32),
        ],
        2 * rows * feats * width,
        12 * MIB,
        heads * rows,
        [pltpu.VMEM((heads, rows), f32)],
    )(log_decay, keys, values)
    got = lax.all_to_all(send, AXES, 0, 0, tiled=True)
    group = 2
    intra = call(
        "intra",
        functools.partial(intra_kernel, group, width, tile),
        group,
        [whole(heads, rows), lines(group * (parts - 1) * width), *[cols(group)] * 3],
        cols(group),
        like(bf16),
        4 * rows * tile * feats,
        18 * MIB,
        heads * rows * tile,
    )(cumul, near, queries, keys, values)
    got, intra = lax.optimization_barrier((got, intra))
    entering = pl.pallas_call(
        functools.partial(scan_kernel, piece),
        out_shape=jax.ShapeDtypeStruct((count, piece, width), f32),
        compiler_params=pltpu.CompilerParams(vmem_limit_bytes=8 * MIB),
        cost_estimate=pl.CostEstimate(
            flops=2 * heads * width * width, bytes_accessed=3 * MIB, transcendentals=0
        ),
        name="scan",
    )(got)
    incoming = lax.all_to_all(entering, AXES, 0, 0, tiled=True).reshape(heads * width, width)
    group = 4
    scaled, gated = call(
        "ready",
        functools.partial(ready_kernel, group, width),
        group,
        [whole(heads, rows), cols(group), cols(group), gain(group)],
        [cols(group), cols(group)],
        [like(bf16), like(bf16)],
        40 * rows * feats,
        16 * MIB,
        2 * rows * feats,
    )(cumul, queries, out_gate, norm_gain.reshape(1, feats))
    incoming, scaled, gated = lax.optimization_barrier((incoming, scaled, gated))
    return call(
        "final",
        functools.partial(final_kernel, group, width),
        group,
        [lines(group * width), *[cols(group)] * 3],
        cols(group),
        like(bf16),
        4 * rows * feats * width,
        17 * MIB,
        rows * feats,
    )(incoming, scaled, intra, gated)


def solution(mesh):
    split = P(AXES, None)
    count = 1
    for axis in AXES:
        count *= mesh.shape[axis]
    return jax.shard_map(
        functools.partial(on_device, count),
        mesh=mesh,
        in_specs=(split, split, split, P(None, AXES), split, P()),
        out_specs=split,
        check_vma=False,
    )
```

```python
import functools

import jax
import jax.numpy as jnp
from jax import lax
from jax.experimental import pallas as pl
from jax.experimental.pallas import tpu as pltpu
from jax.sharding import PartitionSpec as P

AXES = ("grp", "seq")
MIB = 1 << 20
LOW = -1e30


def running_sum(decay):
    heads, rows = decay.shape
    a = lax.broadcasted_iota(jnp.int32, (128, 128), 0)
    b = lax.broadcasted_iota(jnp.int32, (128, 128), 1)
    upper = (a <= b).astype(jnp.float32)
    carry = jnp.zeros((heads, 1), jnp.float32)
    parts = []
    for c in range(rows // 128):
        part = jnp.dot(
            decay[:, c * 128 : (c + 1) * 128],
            upper,
            precision=lax.Precision.HIGHEST,
            preferred_element_type=jnp.float32,
        )
        part = part + carry
        carry = part[:, 127:128]
        parts.append(part)
    return jnp.concatenate(parts, axis=1)


def across(first, second):
    zero = jnp.zeros_like(first)
    return jnp.concatenate(
        [jnp.concatenate([first, zero], axis=1), jnp.concatenate([zero, second], axis=1)], axis=0
    )


def fetch(source, target, sems, chunks):
    wide = source.shape[1] // chunks
    return [
        pltpu.make_async_copy(
            source.at[:, pl.ds(c * wide, wide)], target.at[:, pl.ds(c * wide, wide)], sems.at[c]
        )
        for c in range(chunks)
    ]


def state_kernel(
    width, piece, tile, chunks, decay_ref, k_far, v_far, send_far, near_far, cumul_far, k_ref, v_ref,
    stage_ref, near_ref, cumul_ref, k_sems, v_sems, sems, near_sems, cumul_sem,
):
    rows, feats = k_ref.shape
    heads = feats // width
    copies = list(zip(fetch(k_far, k_ref, k_sems, chunks), fetch(v_far, v_ref, v_sems, chunks)))
    ahead = 4
    for pair in copies[:ahead]:
        for copy in pair:
            copy.start()
    cumul = running_sum(decay_ref[...])
    cumul_ref[...] = cumul
    cumul_copy = pltpu.make_async_copy(cumul_ref, cumul_far, cumul_sem)
    cumul_copy.start()

    group = heads // chunks
    per = width // piece
    pairs = piece // 2 + 1
    parts = rows // tile
    sent = []
    for c in range(chunks):
        for copy in copies[c]:
            copy.wait()
        if c + ahead < chunks:
            for copy in copies[c + ahead]:
                copy.start()
        for i in range(c * group, (c + 1) * group):
            row = cumul[i : i + 1, :]
            cut = slice(i * width, (i + 1) * width)
            before = jnp.zeros((1, 1), jnp.float32)
            state = None
            for t in range(parts):
                mine = slice(t * tile, (t + 1) * tile)
                total = row[:, (t + 1) * tile - 1 : (t + 1) * tile]
                scale = jnp.exp(total - row[:, mine])
                keys = k_ref[mine, cut].T.astype(jnp.float32)
                scaled = (keys * scale).astype(jnp.bfloat16)
                fresh = jnp.dot(scaled, v_ref[mine, cut], preferred_element_type=jnp.float32)
                state = fresh if t == 0 else state * jnp.exp(total - before) + fresh
                before = total
                if t < parts - 1:
                    at = (i * (parts - 1) + t) * width
                    near_ref[at : at + width, :] = state.astype(jnp.bfloat16)
            factor = jnp.broadcast_to(jnp.exp(total), (2, width))
            for p in range(per):
                at = (i * per + p) * pairs
                for r in range(pairs - 1):
                    from_row = p * piece + 2 * r
                    stage_ref[at + r, :, :] = state[from_row : from_row + 2, :]
                stage_ref[at + pairs - 1, :, :] = factor
        for held, far, sem, each in (
            (stage_ref, send_far, sems, group * per * pairs),
            (near_ref, near_far, near_sems, group * (parts - 1) * width),
        ):
            some = pl.ds(c * each, each)
            copy = pltpu.make_async_copy(held.at[some], far.at[some], sem.at[c])
            copy.start()
            sent.append(copy)
    cumul_copy.wait()
    for copy in sent:
        copy.wait()


def scan_kernel(pairs, got_ref, out_ref):
    count = out_ref.shape[0]
    width = got_ref.shape[2]

    def lap(j, carry):
        at = j * pairs
        factor = got_ref[at + pairs - 1]
        for r in range(pairs - 1):
            out_ref[j, 2 * r : 2 * r + 2, :] = carry[r]
        return tuple(carry[r] * factor + got_ref[at + r] for r in range(pairs - 1))

    zero = jnp.zeros((2, width), jnp.float32)
    lax.fori_loop(0, count, lap, (zero,) * (pairs - 1), unroll=8)


def intra_kernel(
    width, tile, chunks, cumul_ref, near_ref, q_far, k_far, v_far, out_far, q_ref, k_ref, v_ref,
    out_ref, q_sems, k_sems, v_sems, sems,
):
    rows, feats = q_ref.shape
    heads = feats // width
    group = heads // chunks
    copies = list(
        zip(
            fetch(q_far, q_ref, q_sems, chunks),
            fetch(k_far, k_ref, k_sems, chunks),
            fetch(v_far, v_ref, v_sems, chunks),
        )
    )
    sent = fetch(out_ref, out_far, sems, chunks)
    for some in copies:
        for copy in some:
            copy.start()
    parts = rows // tile
    a = lax.broadcasted_iota(jnp.int32, (tile, tile), 0)
    b = lax.broadcasted_iota(jnp.int32, (tile, tile), 1)
    mask = jnp.where(a >= b, 0.0, LOW)
    columns = jnp.concatenate(
        [cumul_ref[...], jnp.zeros((width - heads, rows), jnp.float32)], axis=0
    ).T
    for i in range(0, heads, 2):
        if i % group == 0:
            for copy in copies[i // group]:
                copy.wait()
        row = [cumul_ref[i + n : i + n + 1, :] for n in range(2)]
        col = [columns[:, i + n : i + n + 1] for n in range(2)]
        both = slice(i * width, (i + 2) * width)
        for t in range(parts):
            start = t * tile
            mine = slice(start, start + tile)
            if t:
                at = [((i + n) * (parts - 1) + t - 1) * width for n in range(2)]
                far = jnp.dot(
                    q_ref[mine, both],
                    across(*(near_ref[x : x + width, :] for x in at)),
                    preferred_element_type=jnp.float32,
                )
            for n in range(2):
                cut = slice((i + n) * width, (i + n + 1) * width)
                scores = lax.dot_general(
                    q_ref[mine, cut],
                    k_ref[mine, cut],
                    (((1,), (1,)), ((), ())),
                    preferred_element_type=jnp.float32,
                )
                gap = col[n][mine] - row[n][:, mine] + mask
                weights = (jnp.exp(gap) * scores).astype(jnp.bfloat16)
                intra = jnp.dot(weights, v_ref[mine, cut], preferred_element_type=jnp.float32)
                if t:
                    edge = row[n][:, start - 1 : start]
                    intra = intra + jnp.exp(col[n][mine] - edge) * far[:, n * width : (n + 1) * width]
                out_ref[mine, cut] = intra.astype(out_ref.dtype)
        if (i + 2) % group == 0:
            sent[i // group].start()
    for copy in sent:
        copy.wait()


def ready_kernel(
    width, chunks, cumul_ref, q_far, gate_far, gain_ref, scaled_far, gated_far, q_ref, gate_ref,
    scaled_ref, gated_ref, q_sems, gate_sems, scaled_sems, gated_sems,
):
    rows, feats = q_ref.shape
    heads = feats // width
    gates = fetch(gate_far, gate_ref, gate_sems, chunks)
    queries = fetch(q_far, q_ref, q_sems, chunks)
    sent = list(
        zip(
            fetch(scaled_ref, scaled_far, scaled_sems, chunks),
            fetch(gated_ref, gated_far, gated_sems, chunks),
        )
    )
    group = heads // chunks
    for c in range(chunks):
        gates[c].start()
        queries[c].start()
    columns = jnp.concatenate(
        [jnp.exp(cumul_ref[...]), jnp.zeros((width - heads, rows), jnp.float32)], axis=0
    ).T
    for i in range(heads):
        if i % group == 0:
            gates[i // group].wait()
            queries[i // group].wait()
        cut = slice(i * width, (i + 1) * width)
        half = gate_ref[:, cut].astype(jnp.float32) * 0.5
        gated_ref[:, cut] = (gain_ref[:, cut] * (half + half * jnp.tanh(half))).astype(gated_ref.dtype)
        scaled = q_ref[:, cut].astype(jnp.float32) * columns[:, i : i + 1]
        scaled_ref[:, cut] = scaled.astype(scaled_ref.dtype)
        if (i + 1) % group == 0:
            for copy in sent[i // group]:
                copy.start()
    for some in sent:
        for copy in some:
            copy.wait()


def final_kernel(
    width, tile, chunks, state_ref, q_far, intra_far, gated_far, out_far, q_ref, intra_ref, gated_ref,
    out_ref, q_sems, intra_sems, gated_sems, sems,
):
    rows, feats = q_ref.shape
    heads = feats // width
    group = heads // chunks
    copies = list(
        zip(
            fetch(q_far, q_ref, q_sems, chunks),
            fetch(intra_far, intra_ref, intra_sems, chunks),
            fetch(gated_far, gated_ref, gated_sems, chunks),
        )
    )
    sent = fetch(out_ref, out_far, sems, chunks)
    for some in copies:
        for copy in some:
            copy.start()
    share = jnp.full((width, width), 1.0 / width, jnp.bfloat16)
    share = across(share, share)
    for i in range(0, heads, 2):
        if i % group == 0:
            for copy in copies[i // group]:
                copy.wait()
        both = slice(i * width, (i + 2) * width)
        state = state_ref[i * width : (i + 2) * width, :].astype(jnp.bfloat16)
        state = across(state[0:width], state[width:])
        for t in range(rows // tile):
            mine = slice(t * tile, (t + 1) * tile)
            mixed = intra_ref[mine, both].astype(jnp.float32) + jnp.dot(
                q_ref[mine, both], state, preferred_element_type=jnp.float32
            )
            power = jnp.dot(
                (mixed * mixed).astype(jnp.bfloat16), share, preferred_element_type=jnp.float32
            )
            out = mixed * lax.rsqrt(power + 1e-6) * gated_ref[mine, both].astype(jnp.float32)
            out_ref[mine, both] = out.astype(jnp.bfloat16)
        if (i + 2) % group == 0:
            sent[i // group].start()
    for copy in sent:
        copy.wait()


def on_device(count, queries, keys, values, log_decay, out_gate, norm_gain):
    rows, feats = queries.shape
    heads = log_decay.shape[0]
    width = feats // heads
    piece = heads * width // count
    tile = 256
    parts = rows // tile
    chunks = 8
    f32, bf16 = jnp.float32, jnp.bfloat16
    here = pl.BlockSpec(memory_space=pltpu.VMEM)
    there = pl.BlockSpec(memory_space=pl.ANY)
    block = (rows, feats)
    sems = pltpu.SemaphoreType.DMA((chunks,))
    held = pltpu.VMEM(block, bf16)
    moved = jax.ShapeDtypeStruct(block, bf16)

    def call(name, body, ins, outs, shapes, flops, bytes_moved, exps, limit, scratch=()):
        return pl.pallas_call(
            body,
            in_specs=ins,
            out_specs=outs,
            out_shape=shapes,
            scratch_shapes=list(scratch),
            compiler_params=pltpu.CompilerParams(vmem_limit_bytes=limit * MIB),
            cost_estimate=pl.CostEstimate(flops=flops, bytes_accessed=bytes_moved, transcendentals=exps),
            name=name,
        )

    pairs = piece // 2 + 1
    message = (count * pairs, 2, width)
    inner = (heads * (parts - 1) * width, width)
    send, near, cumul = call(
        "states",
        functools.partial(state_kernel, width, piece, tile, chunks),
        [here, there, there],
        [there, there, there],
        [
            jax.ShapeDtypeStruct(message, f32),
            jax.ShapeDtypeStruct(inner, bf16),
            jax.ShapeDtypeStruct((heads, rows), f32),
        ],
        2 * rows * feats * width,
        12 * MIB,
        heads * rows,
        56,
        [
            held,
            held,
            pltpu.VMEM(message, f32),
            pltpu.VMEM(inner, bf16),
            pltpu.VMEM((heads, rows), f32),
            *[sems] * 4,
            pltpu.SemaphoreType.DMA,
        ],
    )(log_decay, keys, values)
    got = lax.all_to_all(send, AXES, 0, 0, tiled=True)
    intra = call(
        "intra",
        functools.partial(intra_kernel, width, tile, chunks),
        [here, here, there, there, there],
        there,
        moved,
        4 * rows * tile * feats,
        18 * MIB,
        heads * rows * tile,
        56,
        [*[held] * 4, *[sems] * 4],
    )(cumul, near, queries, keys, values)
    got, intra = lax.optimization_barrier((got, intra))
    entering = call(
        "scan",
        functools.partial(scan_kernel, pairs),
        [here],
        here,
        jax.ShapeDtypeStruct((count, piece, width), f32),
        2 * heads * width * width,
        3 * MIB,
        0,
        8,
    )(got)
    incoming = lax.all_to_all(entering, AXES, 0, 0, tiled=True).reshape(heads * width, width)
    scaled, gated = call(
        "ready",
        functools.partial(ready_kernel, width, chunks),
        [here, there, there, here],
        [there, there],
        [moved, moved],
        40 * rows * feats,
        16 * MIB,
        2 * rows * feats,
        56,
        [*[held] * 4, *[sems] * 4],
    )(cumul, queries, out_gate, norm_gain.reshape(1, feats))
    incoming, scaled, gated = lax.optimization_barrier((incoming, scaled, gated))
    return call(
        "final",
        functools.partial(final_kernel, width, 128, chunks),
        [here, there, there, there],
        there,
        moved,
        4 * rows * feats * width,
        17 * MIB,
        rows * feats,
        52,
        [*[held] * 4, *[sems] * 4],
    )(incoming, scaled, intra, gated)


def solution(mesh):
    split = P(AXES, None)
    count = 1
    for axis in AXES:
        count *= mesh.shape[axis]
    return jax.shard_map(
        functools.partial(on_device, count),
        mesh=mesh,
        in_specs=(split, split, split, P(None, AXES), split, P()),
        out_specs=split,
        check_vma=False,
    )
```

```python
import functools

import jax
import jax.numpy as jnp
from jax import lax
from jax.experimental import pallas as pl
from jax.experimental.pallas import tpu as pltpu
from jax.sharding import PartitionSpec as P

AXES = ("grp", "seq")
MIB = 1 << 20
LOW = -1e30


def running_sum(decay):
    heads, rows = decay.shape
    a = lax.broadcasted_iota(jnp.int32, (128, 128), 0)
    b = lax.broadcasted_iota(jnp.int32, (128, 128), 1)
    upper = (a <= b).astype(jnp.float32)
    pieces = [decay[:, c * 128 : (c + 1) * 128] for c in range(rows // 128)]
    sums = jnp.dot(
        jnp.concatenate(pieces, axis=0),
        upper,
        precision=lax.Precision.HIGHEST,
        preferred_element_type=jnp.float32,
    )
    carry = jnp.zeros((heads, 1), jnp.float32)
    parts = []
    for c in range(rows // 128):
        part = sums[c * heads : (c + 1) * heads] + carry
        carry = part[:, 127:128]
        parts.append(part)
    return jnp.concatenate(parts, axis=1)


def across(first, second):
    zero = jnp.zeros_like(first)
    return jnp.concatenate(
        [jnp.concatenate([first, zero], axis=1), jnp.concatenate([zero, second], axis=1)], axis=0
    )


def fetch(source, target, sems, chunks):
    wide = source.shape[1] // chunks
    return [
        pltpu.make_async_copy(
            source.at[:, pl.ds(c * wide, wide)], target.at[:, pl.ds(c * wide, wide)], sems.at[c]
        )
        for c in range(chunks)
    ]


def state_kernel(
    width, piece, tile, chunks, decay_ref, k_far, v_far, send_far, near_far, cumul_far, k_ref, v_ref,
    stage_ref, near_ref, cumul_ref, k_sems, v_sems, sems, near_sems, cumul_sem,
):
    rows, feats = k_ref.shape
    heads = feats // width
    copies = list(zip(fetch(k_far, k_ref, k_sems, chunks), fetch(v_far, v_ref, v_sems, chunks)))
    ahead = 4
    for pair in copies[:ahead]:
        for copy in pair:
            copy.start()
    cumul = running_sum(decay_ref[...])
    cumul_ref[...] = cumul
    cumul_copy = pltpu.make_async_copy(cumul_ref, cumul_far, cumul_sem)
    cumul_copy.start()

    group = heads // chunks
    per = width // piece
    pairs = piece // 2 + 1
    parts = rows // tile
    sent = []
    for c in range(chunks):
        for copy in copies[c]:
            copy.wait()
        if c + ahead < chunks:
            for copy in copies[c + ahead]:
                copy.start()
        for i in range(c * group, (c + 1) * group):
            row = cumul[i : i + 1, :]
            cut = slice(i * width, (i + 1) * width)
            before = jnp.zeros((1, 1), jnp.float32)
            state = None
            for t in range(parts):
                mine = slice(t * tile, (t + 1) * tile)
                total = row[:, (t + 1) * tile - 1 : (t + 1) * tile]
                scale = jnp.exp(total - row[:, mine])
                keys = k_ref[mine, cut].T.astype(jnp.float32)
                scaled = (keys * scale).astype(jnp.bfloat16)
                fresh = jnp.dot(scaled, v_ref[mine, cut], preferred_element_type=jnp.float32)
                state = fresh if t == 0 else state * jnp.exp(total - before) + fresh
                before = total
                if t < parts - 1:
                    at = (i * (parts - 1) + t) * width
                    near_ref[at : at + width, :] = state.astype(jnp.bfloat16)
            factor = jnp.broadcast_to(jnp.exp(total), (2, width))
            for p in range(per):
                at = (i * per + p) * pairs
                for r in range(pairs - 1):
                    from_row = p * piece + 2 * r
                    stage_ref[at + r, :, :] = state[from_row : from_row + 2, :]
                stage_ref[at + pairs - 1, :, :] = factor
        for held, far, sem, each in (
            (stage_ref, send_far, sems, group * per * pairs),
            (near_ref, near_far, near_sems, group * (parts - 1) * width),
        ):
            some = pl.ds(c * each, each)
            copy = pltpu.make_async_copy(held.at[some], far.at[some], sem.at[c])
            copy.start()
            sent.append(copy)
    cumul_copy.wait()
    for copy in sent:
        copy.wait()


def scan_kernel(pairs, chunks, got_ref, out_far, out_ref, sems):
    count = out_ref.shape[0]
    width = got_ref.shape[2]

    def lap(j, carry):
        at = j * pairs
        factor = got_ref[at + pairs - 1]
        for r in range(pairs - 1):
            out_ref[j, 2 * r : 2 * r + 2, :] = carry[r]
        return tuple(carry[r] * factor + got_ref[at + r] for r in range(pairs - 1))

    carry = (jnp.zeros((2, width), jnp.float32),) * (pairs - 1)
    each = count // chunks
    sent = []
    for c in range(chunks):
        carry = lax.fori_loop(c * each, (c + 1) * each, lap, carry, unroll=8)
        some = pl.ds(c * each, each)
        copy = pltpu.make_async_copy(out_ref.at[some], out_far.at[some], sems.at[c])
        copy.start()
        sent.append(copy)
    for copy in sent:
        copy.wait()


def intra_kernel(
    width, tile, chunks, cumul_ref, near_ref, q_far, k_far, v_far, out_far, q_ref, k_ref, v_ref,
    out_ref, q_sems, k_sems, v_sems, sems,
):
    rows, feats = q_ref.shape
    heads = feats // width
    group = heads // chunks
    copies = list(
        zip(
            fetch(q_far, q_ref, q_sems, chunks),
            fetch(k_far, k_ref, k_sems, chunks),
            fetch(v_far, v_ref, v_sems, chunks),
        )
    )
    sent = fetch(out_ref, out_far, sems, chunks)
    for some in copies:
        for copy in some:
            copy.start()
    parts = rows // tile
    a = lax.broadcasted_iota(jnp.int32, (tile, tile), 0)
    b = lax.broadcasted_iota(jnp.int32, (tile, tile), 1)
    mask = jnp.where(a >= b, 0.0, LOW)
    columns = jnp.concatenate(
        [cumul_ref[...], jnp.zeros((width - heads, rows), jnp.float32)], axis=0
    ).T
    for i in range(0, heads, 2):
        if i % group == 0:
            for copy in copies[i // group]:
                copy.wait()
        row = [cumul_ref[i + n : i + n + 1, :] for n in range(2)]
        col = [columns[:, i + n : i + n + 1] for n in range(2)]
        both = slice(i * width, (i + 2) * width)
        for t in range(parts):
            start = t * tile
            mine = slice(start, start + tile)
            if t:
                at = [((i + n) * (parts - 1) + t - 1) * width for n in range(2)]
                far = jnp.dot(
                    q_ref[mine, both],
                    across(*(near_ref[x : x + width, :] for x in at)),
                    preferred_element_type=jnp.float32,
                )
            for n in range(2):
                cut = slice((i + n) * width, (i + n + 1) * width)
                scores = lax.dot_general(
                    q_ref[mine, cut],
                    k_ref[mine, cut],
                    (((1,), (1,)), ((), ())),
                    preferred_element_type=jnp.float32,
                )
                gap = col[n][mine] - row[n][:, mine] + mask
                weights = (jnp.exp(gap) * scores).astype(jnp.bfloat16)
                intra = jnp.dot(weights, v_ref[mine, cut], preferred_element_type=jnp.float32)
                if t:
                    edge = row[n][:, start - 1 : start]
                    intra = intra + jnp.exp(col[n][mine] - edge) * far[:, n * width : (n + 1) * width]
                out_ref[mine, cut] = intra.astype(out_ref.dtype)
        if (i + 2) % group == 0:
            sent[i // group].start()
    for copy in sent:
        copy.wait()


def ready_kernel(
    width, chunks, cumul_ref, q_far, gate_far, gain_ref, scaled_far, gated_far, q_ref, gate_ref,
    scaled_ref, gated_ref, q_sems, gate_sems, scaled_sems, gated_sems,
):
    rows, feats = q_ref.shape
    heads = feats // width
    gates = fetch(gate_far, gate_ref, gate_sems, chunks)
    queries = fetch(q_far, q_ref, q_sems, chunks)
    sent = list(
        zip(
            fetch(scaled_ref, scaled_far, scaled_sems, chunks),
            fetch(gated_ref, gated_far, gated_sems, chunks),
        )
    )
    group = heads // chunks
    for c in range(chunks):
        gates[c].start()
        queries[c].start()
    columns = jnp.concatenate(
        [jnp.exp(cumul_ref[...]), jnp.zeros((width - heads, rows), jnp.float32)], axis=0
    ).T
    for i in range(heads):
        if i % group == 0:
            gates[i // group].wait()
            queries[i // group].wait()
        cut = slice(i * width, (i + 1) * width)
        half = gate_ref[:, cut].astype(jnp.float32) * 0.5
        gated_ref[:, cut] = (gain_ref[:, cut] * (half + half * jnp.tanh(half))).astype(gated_ref.dtype)
        scaled = q_ref[:, cut].astype(jnp.float32) * columns[:, i : i + 1]
        scaled_ref[:, cut] = scaled.astype(scaled_ref.dtype)
        if (i + 1) % group == 0:
            for copy in sent[i // group]:
                copy.start()
    for some in sent:
        for copy in some:
            copy.wait()


def final_kernel(
    width, tile, chunks, state_ref, q_far, intra_far, gated_far, out_far, q_ref, intra_ref, gated_ref,
    out_ref, q_sems, intra_sems, gated_sems, sems,
):
    rows, feats = q_ref.shape
    heads = feats // width
    group = heads // chunks
    copies = list(
        zip(
            fetch(q_far, q_ref, q_sems, chunks),
            fetch(intra_far, intra_ref, intra_sems, chunks),
            fetch(gated_far, gated_ref, gated_sems, chunks),
        )
    )
    sent = fetch(out_ref, out_far, sems, chunks)
    for some in copies:
        for copy in some:
            copy.start()
    share = jnp.full((width, width), 1.0 / width, jnp.bfloat16)
    share = across(share, share)
    for i in range(0, heads, 2):
        if i % group == 0:
            for copy in copies[i // group]:
                copy.wait()
        both = slice(i * width, (i + 2) * width)
        state = state_ref[i * width : (i + 2) * width, :].astype(jnp.bfloat16)
        state = across(state[0:width], state[width:])
        for t in range(rows // tile):
            mine = slice(t * tile, (t + 1) * tile)
            mixed = intra_ref[mine, both].astype(jnp.float32) + jnp.dot(
                q_ref[mine, both], state, preferred_element_type=jnp.float32
            )
            power = jnp.dot(
                (mixed * mixed).astype(jnp.bfloat16), share, preferred_element_type=jnp.float32
            )
            out = mixed * lax.rsqrt(power + 1e-6) * gated_ref[mine, both].astype(jnp.float32)
            out_ref[mine, both] = out.astype(jnp.bfloat16)
        if (i + 2) % group == 0:
            sent[i // group].start()
    for copy in sent:
        copy.wait()


def on_device(count, queries, keys, values, log_decay, out_gate, norm_gain):
    rows, feats = queries.shape
    heads = log_decay.shape[0]
    width = feats // heads
    piece = heads * width // count
    tile = 256
    parts = rows // tile
    chunks, few = 8, 4
    f32, bf16 = jnp.float32, jnp.bfloat16
    here = pl.BlockSpec(memory_space=pltpu.VMEM)
    there = pl.BlockSpec(memory_space=pl.ANY)
    block = (rows, feats)
    sems = pltpu.SemaphoreType.DMA((chunks,))
    few_sems = pltpu.SemaphoreType.DMA((few,))
    held = pltpu.VMEM(block, bf16)
    moved = jax.ShapeDtypeStruct(block, bf16)

    def call(name, body, ins, outs, shapes, flops, bytes_moved, exps, limit, scratch=()):
        return pl.pallas_call(
            body,
            in_specs=ins,
            out_specs=outs,
            out_shape=shapes,
            scratch_shapes=list(scratch),
            compiler_params=pltpu.CompilerParams(vmem_limit_bytes=limit * MIB),
            cost_estimate=pl.CostEstimate(flops=flops, bytes_accessed=bytes_moved, transcendentals=exps),
            name=name,
        )

    pairs = piece // 2 + 1
    message = (count * pairs, 2, width)
    inner = (heads * (parts - 1) * width, width)
    send, near, cumul = call(
        "states",
        functools.partial(state_kernel, width, piece, tile, few),
        [here, there, there],
        [there, there, there],
        [
            jax.ShapeDtypeStruct(message, f32),
            jax.ShapeDtypeStruct(inner, bf16),
            jax.ShapeDtypeStruct((heads, rows), f32),
        ],
        2 * rows * feats * width,
        12 * MIB,
        heads * rows,
        56,
        [
            held,
            held,
            pltpu.VMEM(message, f32),
            pltpu.VMEM(inner, bf16),
            pltpu.VMEM((heads, rows), f32),
            *[few_sems] * 4,
            pltpu.SemaphoreType.DMA,
        ],
    )(log_decay, keys, values)
    got = lax.all_to_all(send, AXES, 0, 0, tiled=True)
    intra = call(
        "intra",
        functools.partial(intra_kernel, width, tile, few),
        [here, here, there, there, there],
        there,
        moved,
        4 * rows * tile * feats,
        18 * MIB,
        heads * rows * tile,
        56,
        [*[held] * 4, *[few_sems] * 4],
    )(cumul, near, queries, keys, values)
    got, intra = lax.optimization_barrier((got, intra))
    entering = call(
        "scan",
        functools.partial(scan_kernel, pairs, few),
        [here],
        there,
        jax.ShapeDtypeStruct((count, piece, width), f32),
        2 * heads * width * width,
        3 * MIB,
        0,
        8,
        [pltpu.VMEM((count, piece, width), f32), few_sems],
    )(got)
    incoming = lax.all_to_all(entering, AXES, 0, 0, tiled=True).reshape(heads * width, width)
    scaled, gated = call(
        "ready",
        functools.partial(ready_kernel, width, chunks),
        [here, there, there, here],
        [there, there],
        [moved, moved],
        40 * rows * feats,
        16 * MIB,
        2 * rows * feats,
        56,
        [*[held] * 4, *[sems] * 4],
    )(cumul, queries, out_gate, norm_gain.reshape(1, feats))
    incoming, scaled, gated = lax.optimization_barrier((incoming, scaled, gated))
    return call(
        "final",
        functools.partial(final_kernel, width, 128, chunks),
        [here, there, there, there],
        there,
        moved,
        4 * rows * feats * width,
        17 * MIB,
        rows * feats,
        52,
        [*[held] * 4, *[sems] * 4],
    )(incoming, scaled, intra, gated)


def solution(mesh):
    split = P(AXES, None)
    count = 1
    for axis in AXES:
        count *= mesh.shape[axis]
    return jax.shard_map(
        functools.partial(on_device, count),
        mesh=mesh,
        in_specs=(split, split, split, P(None, AXES), split, P()),
        out_specs=split,
        check_vma=False,
    )
```

```python
import functools

import jax
import jax.numpy as jnp
from jax import lax
from jax.experimental import pallas as pl
from jax.experimental.pallas import tpu as pltpu
from jax.sharding import PartitionSpec as P

AXES = ("grp", "seq")
MIB = 1 << 20
LOW = -1e30


def running_sum(decay):
    heads, rows = decay.shape
    a = lax.broadcasted_iota(jnp.int32, (128, 128), 0)
    b = lax.broadcasted_iota(jnp.int32, (128, 128), 1)
    upper = (a <= b).astype(jnp.float32)
    pieces = [decay[:, c * 128 : (c + 1) * 128] for c in range(rows // 128)]
    sums = jnp.dot(
        jnp.concatenate(pieces, axis=0),
        upper,
        precision=lax.Precision.HIGHEST,
        preferred_element_type=jnp.float32,
    )
    carry = jnp.zeros((heads, 1), jnp.float32)
    parts = []
    for c in range(rows // 128):
        part = sums[c * heads : (c + 1) * heads] + carry
        carry = part[:, 127:128]
        parts.append(part)
    return jnp.concatenate(parts, axis=1)


def across(first, second):
    zero = jnp.zeros_like(first)
    return jnp.concatenate(
        [jnp.concatenate([first, zero], axis=1), jnp.concatenate([zero, second], axis=1)], axis=0
    )


def fetch(source, target, sems, heads, width):
    edges = borders(heads)
    return [
        pltpu.make_async_copy(
            source.at[:, pl.ds(first * width, (last - first) * width)],
            target.at[:, pl.ds(first * width, (last - first) * width)],
            sems.at[c],
        )
        for c, (first, last) in enumerate(zip(edges, edges[1:]))
    ]


def borders(heads):
    small, large = heads // 8, heads // 4
    return [0, *(small + n * large for n in range(4)), heads]


def state_kernel(
    width, piece, tile, chunks, decay_ref, k_far, v_far, send_far, near_far, cumul_far, k_ref, v_ref,
    stage_ref, near_ref, cumul_ref, k_sems, v_sems, sems, near_sems, cumul_sem,
):
    rows, feats = k_ref.shape
    heads = feats // width
    copies = list(zip(fetch(k_far, k_ref, k_sems, heads, width), fetch(v_far, v_ref, v_sems, heads, width)))
    for pair in copies:
        for copy in pair:
            copy.start()
    cumul = running_sum(decay_ref[...])
    cumul_ref[...] = cumul
    cumul_copy = pltpu.make_async_copy(cumul_ref, cumul_far, cumul_sem)
    cumul_copy.start()

    edges = borders(heads)
    per = width // piece
    pairs = piece // 2 + 1
    parts = rows // tile
    sent = []
    for c, (first, last) in enumerate(zip(edges, edges[1:])):
        for copy in copies[c]:
            copy.wait()
        for i in range(first, last):
            row = cumul[i : i + 1, :]
            cut = slice(i * width, (i + 1) * width)
            before = jnp.zeros((1, 1), jnp.float32)
            state = None
            for t in range(parts):
                mine = slice(t * tile, (t + 1) * tile)
                total = row[:, (t + 1) * tile - 1 : (t + 1) * tile]
                scale = jnp.exp(total - row[:, mine])
                keys = k_ref[mine, cut].T.astype(jnp.float32)
                scaled = (keys * scale).astype(jnp.bfloat16)
                fresh = jnp.dot(scaled, v_ref[mine, cut], preferred_element_type=jnp.float32)
                state = fresh if t == 0 else state * jnp.exp(total - before) + fresh
                before = total
                if t < parts - 1:
                    at = (i * (parts - 1) + t) * width
                    near_ref[at : at + width, :] = state.astype(jnp.bfloat16)
            factor = jnp.broadcast_to(jnp.exp(total), (2, width))
            for p in range(per):
                at = (i * per + p) * pairs
                for r in range(pairs - 1):
                    from_row = p * piece + 2 * r
                    stage_ref[at + r, :, :] = state[from_row : from_row + 2, :]
                stage_ref[at + pairs - 1, :, :] = factor
        for held, far, sem, each in (
            (stage_ref, send_far, sems, per * pairs),
            (near_ref, near_far, near_sems, (parts - 1) * width),
        ):
            some = pl.ds(first * each, (last - first) * each)
            copy = pltpu.make_async_copy(held.at[some], far.at[some], sem.at[c])
            copy.start()
            sent.append(copy)
    cumul_copy.wait()
    for copy in sent:
        copy.wait()


def scan_kernel(pairs, chunks, got_ref, out_far, out_ref, sems):
    count = out_ref.shape[0]
    width = got_ref.shape[2]

    def lap(j, carry):
        at = j * pairs
        factor = got_ref[at + pairs - 1]
        for r in range(pairs - 1):
            out_ref[j, 2 * r : 2 * r + 2, :] = carry[r]
        return tuple(carry[r] * factor + got_ref[at + r] for r in range(pairs - 1))

    carry = (jnp.zeros((2, width), jnp.float32),) * (pairs - 1)
    each = count // chunks
    sent = []
    for c in range(chunks):
        carry = lax.fori_loop(c * each, (c + 1) * each, lap, carry, unroll=8)
        some = pl.ds(c * each, each)
        copy = pltpu.make_async_copy(out_ref.at[some], out_far.at[some], sems.at[c])
        copy.start()
        sent.append(copy)
    for copy in sent:
        copy.wait()


def intra_kernel(
    width, tile, chunks, cumul_ref, near_ref, q_far, k_far, v_far, out_far, q_ref, k_ref, v_ref,
    out_ref, q_sems, k_sems, v_sems, sems,
):
    rows, feats = q_ref.shape
    heads = feats // width
    edges = borders(heads)
    copies = list(
        zip(
            fetch(q_far, q_ref, q_sems, heads, width),
            fetch(k_far, k_ref, k_sems, heads, width),
            fetch(v_far, v_ref, v_sems, heads, width),
        )
    )
    sent = fetch(out_ref, out_far, sems, heads, width)
    for some in copies:
        for copy in some:
            copy.start()
    parts = rows // tile
    a = lax.broadcasted_iota(jnp.int32, (tile, tile), 0)
    b = lax.broadcasted_iota(jnp.int32, (tile, tile), 1)
    mask = jnp.where(a >= b, 0.0, LOW)
    columns = jnp.concatenate(
        [cumul_ref[...], jnp.zeros((width - heads, rows), jnp.float32)], axis=0
    ).T
    for i in range(0, heads, 2):
        if i in edges:
            for copy in copies[edges.index(i)]:
                copy.wait()
        row = [cumul_ref[i + n : i + n + 1, :] for n in range(2)]
        col = [columns[:, i + n : i + n + 1] for n in range(2)]
        both = slice(i * width, (i + 2) * width)
        for t in range(parts):
            start = t * tile
            mine = slice(start, start + tile)
            if t:
                at = [((i + n) * (parts - 1) + t - 1) * width for n in range(2)]
                far = jnp.dot(
                    q_ref[mine, both],
                    across(*(near_ref[x : x + width, :] for x in at)),
                    preferred_element_type=jnp.float32,
                )
            for n in range(2):
                cut = slice((i + n) * width, (i + n + 1) * width)
                scores = lax.dot_general(
                    q_ref[mine, cut],
                    k_ref[mine, cut],
                    (((1,), (1,)), ((), ())),
                    preferred_element_type=jnp.float32,
                )
                gap = col[n][mine] - row[n][:, mine] + mask
                weights = (jnp.exp(gap) * scores).astype(jnp.bfloat16)
                intra = jnp.dot(weights, v_ref[mine, cut], preferred_element_type=jnp.float32)
                if t:
                    edge = row[n][:, start - 1 : start]
                    intra = intra + jnp.exp(col[n][mine] - edge) * far[:, n * width : (n + 1) * width]
                out_ref[mine, cut] = intra.astype(out_ref.dtype)
        if i + 2 in edges:
            sent[edges.index(i + 2) - 1].start()
    for copy in sent:
        copy.wait()


def ready_kernel(
    width, chunks, cumul_ref, q_far, gate_far, gain_ref, scaled_far, gated_far, q_ref, gate_ref,
    scaled_ref, gated_ref, q_sems, gate_sems, scaled_sems, gated_sems,
):
    rows, feats = q_ref.shape
    heads = feats // width
    gates = fetch(gate_far, gate_ref, gate_sems, heads, width)
    queries = fetch(q_far, q_ref, q_sems, heads, width)
    sent = list(
        zip(
            fetch(scaled_ref, scaled_far, scaled_sems, heads, width),
            fetch(gated_ref, gated_far, gated_sems, heads, width),
        )
    )
    edges = borders(heads)
    for pair in zip(gates, queries):
        for copy in pair:
            copy.start()
    columns = jnp.concatenate(
        [jnp.exp(cumul_ref[...]), jnp.zeros((width - heads, rows), jnp.float32)], axis=0
    ).T
    for i in range(heads):
        if i in edges:
            gates[edges.index(i)].wait()
            queries[edges.index(i)].wait()
        cut = slice(i * width, (i + 1) * width)
        half = gate_ref[:, cut].astype(jnp.float32) * 0.5
        gated_ref[:, cut] = (gain_ref[:, cut] * (half + half * jnp.tanh(half))).astype(gated_ref.dtype)
        scaled = q_ref[:, cut].astype(jnp.float32) * columns[:, i : i + 1]
        scaled_ref[:, cut] = scaled.astype(scaled_ref.dtype)
        if i + 1 in edges:
            for copy in sent[edges.index(i + 1) - 1]:
                copy.start()
    for some in sent:
        for copy in some:
            copy.wait()


def final_kernel(
    width, tile, chunks, state_ref, q_far, intra_far, gated_far, out_far, q_ref, intra_ref, gated_ref,
    out_ref, q_sems, intra_sems, gated_sems, sems,
):
    rows, feats = q_ref.shape
    heads = feats // width
    edges = borders(heads)
    copies = list(
        zip(
            fetch(q_far, q_ref, q_sems, heads, width),
            fetch(intra_far, intra_ref, intra_sems, heads, width),
            fetch(gated_far, gated_ref, gated_sems, heads, width),
        )
    )
    sent = fetch(out_ref, out_far, sems, heads, width)
    for some in copies:
        for copy in some:
            copy.start()
    share = jnp.full((width, width), 1.0 / width, jnp.bfloat16)
    share = across(share, share)
    for i in range(0, heads, 2):
        if i in edges:
            for copy in copies[edges.index(i)]:
                copy.wait()
        both = slice(i * width, (i + 2) * width)
        state = state_ref[i * width : (i + 2) * width, :].astype(jnp.bfloat16)
        state = across(state[0:width], state[width:])
        for t in range(rows // tile):
            mine = slice(t * tile, (t + 1) * tile)
            mixed = intra_ref[mine, both].astype(jnp.float32) + jnp.dot(
                q_ref[mine, both], state, preferred_element_type=jnp.float32
            )
            power = jnp.dot(
                (mixed * mixed).astype(jnp.bfloat16), share, preferred_element_type=jnp.float32
            )
            out = mixed * lax.rsqrt(power + 1e-6) * gated_ref[mine, both].astype(jnp.float32)
            out_ref[mine, both] = out.astype(jnp.bfloat16)
        if i + 2 in edges:
            sent[edges.index(i + 2) - 1].start()
    for copy in sent:
        copy.wait()


def on_device(count, queries, keys, values, log_decay, out_gate, norm_gain):
    rows, feats = queries.shape
    heads = log_decay.shape[0]
    width = feats // heads
    piece = heads * width // count
    tile = 256
    parts = rows // tile
    chunks, few = 8, 4
    f32, bf16 = jnp.float32, jnp.bfloat16
    here = pl.BlockSpec(memory_space=pltpu.VMEM)
    there = pl.BlockSpec(memory_space=pl.ANY)
    block = (rows, feats)
    sems = pltpu.SemaphoreType.DMA((len(borders(heads)) - 1,))
    few_sems = pltpu.SemaphoreType.DMA((few,))
    held = pltpu.VMEM(block, bf16)
    moved = jax.ShapeDtypeStruct(block, bf16)

    def call(name, body, ins, outs, shapes, flops, bytes_moved, exps, limit, scratch=()):
        return pl.pallas_call(
            body,
            in_specs=ins,
            out_specs=outs,
            out_shape=shapes,
            scratch_shapes=list(scratch),
            compiler_params=pltpu.CompilerParams(vmem_limit_bytes=limit * MIB),
            cost_estimate=pl.CostEstimate(flops=flops, bytes_accessed=bytes_moved, transcendentals=exps),
            name=name,
        )

    pairs = piece // 2 + 1
    message = (count * pairs, 2, width)
    inner = (heads * (parts - 1) * width, width)
    send, near, cumul = call(
        "states",
        functools.partial(state_kernel, width, piece, tile, few),
        [here, there, there],
        [there, there, there],
        [
            jax.ShapeDtypeStruct(message, f32),
            jax.ShapeDtypeStruct(inner, bf16),
            jax.ShapeDtypeStruct((heads, rows), f32),
        ],
        2 * rows * feats * width,
        12 * MIB,
        heads * rows,
        56,
        [
            held,
            held,
            pltpu.VMEM(message, f32),
            pltpu.VMEM(inner, bf16),
            pltpu.VMEM((heads, rows), f32),
            *[sems] * 4,
            pltpu.SemaphoreType.DMA,
        ],
    )(log_decay, keys, values)
    got = lax.all_to_all(send, AXES, 0, 0, tiled=True)
    intra = call(
        "intra",
        functools.partial(intra_kernel, width, tile, few),
        [here, here, there, there, there],
        there,
        moved,
        4 * rows * tile * feats,
        18 * MIB,
        heads * rows * tile,
        56,
        [*[held] * 4, *[sems] * 4],
    )(cumul, near, queries, keys, values)
    got, intra = lax.optimization_barrier((got, intra))
    entering = call(
        "scan",
        functools.partial(scan_kernel, pairs, few),
        [here],
        there,
        jax.ShapeDtypeStruct((count, piece, width), f32),
        2 * heads * width * width,
        3 * MIB,
        0,
        8,
        [pltpu.VMEM((count, piece, width), f32), few_sems],
    )(got)
    incoming = lax.all_to_all(entering, AXES, 0, 0, tiled=True).reshape(heads * width, width)
    scaled, gated = call(
        "ready",
        functools.partial(ready_kernel, width, chunks),
        [here, there, there, here],
        [there, there],
        [moved, moved],
        40 * rows * feats,
        16 * MIB,
        2 * rows * feats,
        56,
        [*[held] * 4, *[sems] * 4],
    )(cumul, queries, out_gate, norm_gain.reshape(1, feats))
    incoming, scaled, gated = lax.optimization_barrier((incoming, scaled, gated))
    return call(
        "final",
        functools.partial(final_kernel, width, 128, chunks),
        [here, there, there, there],
        there,
        moved,
        4 * rows * feats * width,
        17 * MIB,
        rows * feats,
        52,
        [*[held] * 4, *[sems] * 4],
    )(incoming, scaled, intra, gated)


def solution(mesh):
    split = P(AXES, None)
    count = 1
    for axis in AXES:
        count *= mesh.shape[axis]
    return jax.shard_map(
        functools.partial(on_device, count),
        mesh=mesh,
        in_specs=(split, split, split, P(None, AXES), split, P()),
        out_specs=split,
        check_vma=False,
    )
```
